32 devices in a mesh: freq: 8 (over z, y), dish: 4 (over x, core).
Axes of the slice: x: 2, y: 2, z: 4, core: 2. Of those that a mesh axis runs over, the one named last changes fastest.
Arguments:
- voltages: bfloat16 [256, 4, 2, 155648], P('freq', 'dish'), may hold values from -6 to 6
- feed_gains: bfloat16 [256, 4, 2, 8192], P('freq', 'dish'), may hold values from -4.1875 to 4.1875
- block_assign: int32 [8], replicated, may hold values from 0 to 7, each once
- grid_rows: int32 [4, 256], replicated, may hold values from 0 to 255, each once within a row
Outputs:
- beam_power: float32 [8192, 1024], P('freq', 'dish')
The draws below stay inside these ranges and needn't reach their ends.
Inputs may be any that keep to these rules, and one draw needn't show every extreme that they name: block_assign names every channel block once. Each row of grid_rows names every grid row once.
All inputs are finite; a program needn't handle non-finite values.
Results may differ from the reference program's by a relative error of at most 0.0042.
Values may be sent and summed in bfloat16 or wider, within the bound.
A program may use at most 192 MiB of HBM per device.

```python
import math
import jax
import jax.numpy as jnp
import numpy as np
from jax import lax

DISHES = 1024
NCHAN = 8192
CHA = 64
CHB = 128
TAPS = 4
FRAMES = 16
GRIDLEN = 256
CBLOCK = 1024
NBLOCKS = 8
SAMPLES = 155648
N_DISH = 4


def steps_of(own_key, shape, pieces, smallest, top_value):
    gain = 1.0
    for dim, blocks in pieces:
        steps = jax.random.uniform(jax.random.fold_in(jax.random.fold_in(own_key, 6), dim), (blocks,), jnp.float32, smallest / len(pieces), top_value / len(pieces))
        gain = gain * jnp.repeat(jnp.exp(steps), shape[dim] // blocks).reshape((-1,) + (1,) * (len(shape) - 1 - dim))
    return gain


def bell_draw(stream_key, dims, width, bound, split=(), kind=jnp.bfloat16):
    values = jax.random.normal(stream_key, dims, jnp.float32) * width
    if len(split) > 0:
        values = steps_of(stream_key, dims, split, -0.22, 0.18) * values
    return jnp.clip(values, min=-bound, max=bound).astype(kind)


def setup_inputs(seed: int = 0) -> dict:
    key_list = jax.random.split(jax.random.key(seed), 5)
    return {
        "voltages": bell_draw(key_list[0], (GRIDLEN, N_DISH, 2, SAMPLES), 1.0, 6.0, ((0, 8), (1, 4))),
        "feed_gains": bell_draw(key_list[1], (GRIDLEN, N_DISH, 2, NCHAN), 0.7, 4.1875, ((0, 8), (1, 4))),
        "block_assign": jax.random.permutation(key_list[2], NBLOCKS).astype(jnp.int32),
        "grid_rows": jax.vmap(lambda own: jax.random.permutation(own, GRIDLEN))(jax.random.split(key_list[3], N_DISH)).reshape((N_DISH, GRIDLEN)).astype(jnp.int32),
    }


full_turn = 2.0 * math.pi

def fourier_table(row_index, col_index, modulus, scaling):
    phases = row_index[:, None] * col_index[None, :] % modulus
    angles = full_turn / modulus * phases.astype(jnp.float32)
    cosine_table = (jnp.cos(angles) * scaling).astype(jnp.bfloat16)
    sine_table = (jnp.sin(angles) * scaling).astype(jnp.bfloat16)
    upper_rows = jnp.stack([cosine_table, -sine_table], axis=1)
    lower_rows = jnp.stack([sine_table, cosine_table], axis=1)
    return jnp.stack([upper_rows, lower_rows], axis=0)

def rotate(real_part, imag_part, angles):
    cosine_part = jnp.cos(angles)
    sine_part = jnp.sin(angles)
    return (real_part * cosine_part - imag_part * sine_part, real_part * sine_part + imag_part * cosine_part)

def filter_window():
    sample_index = jnp.arange(TAPS * NCHAN, dtype=jnp.float32)
    centred = (sample_index - TAPS * NCHAN / 2 + 0.5) / NCHAN
    taper_curve = 0.5 - 0.5 * jnp.cos(full_turn * (sample_index + 0.5) / (TAPS * NCHAN))
    shaped_window = (jnp.sinc(centred) * taper_curve).reshape(TAPS, NCHAN)
    energy = jnp.mean(lax.optimization_barrier(jnp.sum(shaped_window * shaped_window, axis=0)))
    return shaped_window / jnp.sqrt(energy)

def channelize(dish_volts, dish_gains):
    dish_rows = dish_volts.shape[0]
    window = filter_window()
    framed = dish_volts.reshape(dish_rows, 2, FRAMES + TAPS - 1, NCHAN).astype(jnp.float32)
    filtered = window[0] * framed[:, :, 0:FRAMES]
    for tap_index in range(1, TAPS):
        filtered = filtered + window[tap_index] * framed[:, :, tap_index:tap_index + FRAMES]
    filtered = filtered.astype(jnp.bfloat16)
    blocks = filtered.reshape(dish_rows, 2, FRAMES, CHA, CHB).astype(jnp.float32)
    first_index = jnp.arange(CHA, dtype=jnp.int32)
    second_index = jnp.arange(CHB, dtype=jnp.int32)
    first_table = fourier_table(first_index, first_index, CHA, 1.0 / math.sqrt(CHA)).astype(jnp.float32)
    section_one = jnp.einsum('rpfab,paqc->rfqcb', blocks, first_table, preferred_element_type=jnp.float32)
    angles = -(full_turn / NCHAN) * (first_index[:, None] * second_index[None, :] % NCHAN).astype(jnp.float32)
    real_part, imag_part = rotate(section_one[:, :, 0], section_one[:, :, 1], angles)
    turned = jnp.stack([real_part, imag_part], axis=2).astype(jnp.bfloat16).astype(jnp.float32)
    second_table = fourier_table(second_index, second_index, CHB, 1.0 / math.sqrt(CHB)).astype(jnp.float32)
    spectrum = jnp.einsum('rfqcb,qbse->rfsec', turned, second_table, preferred_element_type=jnp.float32)
    spectrum = spectrum.reshape(dish_rows, FRAMES, 2, NCHAN)
    gain_real = dish_gains[:, 0][:, None, :].astype(jnp.float32)
    gain_imag = dish_gains[:, 1][:, None, :].astype(jnp.float32)
    spectrum_real = spectrum[:, :, 0]
    spectrum_imag = spectrum[:, :, 1]
    out_real = spectrum_real * gain_real - spectrum_imag * gain_imag
    out_imag = spectrum_real * gain_imag + spectrum_imag * gain_real
    return jnp.stack([out_real, out_imag], axis=2).astype(jnp.bfloat16)

def reference(voltages, feed_gains, block_assign, grid_rows):

    def channel_group(members):
        return channelize(members[0], members[1])
    channelized = lax.map(channel_group, (voltages, feed_gains))
    dish_count = N_DISH
    grid_len = GRIDLEN
    positions = jnp.arange(grid_len, dtype=jnp.int32)

    def grid_table(grid_line):
        return fourier_table(grid_line, positions, grid_len, 1.0 / math.sqrt(grid_len))
    tables = jax.vmap(grid_table)(grid_rows).astype(jnp.float32)
    feed_index = jnp.arange(dish_count, dtype=jnp.int32)
    twist_angles = -(full_turn / DISHES) * (feed_index[:, None] * positions[None, :] % DISHES).astype(jnp.float32)
    cross_phases = full_turn / dish_count * (feed_index[:, None] * feed_index[None, :] % dish_count).astype(jnp.float32)
    cross_cos = jnp.cos(cross_phases) / math.sqrt(dish_count)
    cross_sin = jnp.sin(cross_phases) / math.sqrt(dish_count)
    bit_count = dish_count.bit_length() - 1
    reversal = np.array([sum(((member >> bit_index & 1) << bit_count - 1 - bit_index for bit_index in range(bit_count))) for member in range(dish_count)], dtype=np.int32)
    highest = lax.Precision.HIGHEST

    def form_beams(block_index):
        start_row = (block_assign[block_index] * CBLOCK).astype(jnp.int32)
        channel_block = lax.dynamic_slice_in_dim(channelized, start_row, CBLOCK, axis=4).astype(jnp.float32)
        local_sums = jnp.einsum('mdfpc,dpmqk->dfcqk', channel_block, tables, preferred_element_type=jnp.float32)
        real_part, imag_part = rotate(local_sums[:, :, :, 0], local_sums[:, :, :, 1], twist_angles[:, None, None, :])
        rounded = jnp.stack([real_part, imag_part], axis=3).astype(jnp.bfloat16)
        partial_value = lax.optimization_barrier(rounded).astype(jnp.float32)
        part_real = partial_value[:, :, :, 0]
        part_imag = partial_value[:, :, :, 1]
        beam_real = jnp.einsum('dk,dfcb->kfcb', cross_cos, part_real, precision=highest) + jnp.einsum('dk,dfcb->kfcb', cross_sin, part_imag, precision=highest)
        beam_imag = jnp.einsum('dk,dfcb->kfcb', cross_cos, part_imag, precision=highest) - jnp.einsum('dk,dfcb->kfcb', cross_sin, part_real, precision=highest)
        beam_power = lax.optimization_barrier(jnp.mean(beam_real * beam_real + beam_imag * beam_imag, axis=1))
        beam_power = beam_power[reversal]
        return jnp.transpose(beam_power, (1, 0, 2)).reshape(CBLOCK, DISHES)
    result = lax.map(form_beams, jnp.arange(NBLOCKS, dtype=jnp.int32))
    return result.reshape(NCHAN, DISHES)
```

```python
import math

import jax
import jax.numpy as jnp
from jax import lax
from jax.experimental import pallas as pl
from jax.experimental.pallas import tpu as pltpu
from jax.sharding import PartitionSpec as P

NCHAN = 8192
CHA = 64
CHB = 128
TAPS = 4
FRAMES = 16
N_DISH = 4
CHUNKS = 4


full_turn = 2.0 * math.pi


def fourier_table(row_index, col_index, modulus, scaling):
    phases = row_index[:, None] * col_index[None, :] % modulus
    angles = full_turn / modulus * phases.astype(jnp.float32)
    cosine_table = (jnp.cos(angles) * scaling).astype(jnp.bfloat16)
    sine_table = (jnp.sin(angles) * scaling).astype(jnp.bfloat16)
    upper_rows = jnp.stack([cosine_table, -sine_table], axis=1)
    lower_rows = jnp.stack([sine_table, cosine_table], axis=1)
    return jnp.stack([upper_rows, lower_rows], axis=0)


def rotate(real_part, imag_part, angles):
    cosine_part = jnp.cos(angles)
    sine_part = jnp.sin(angles)
    return (
        real_part * cosine_part - imag_part * sine_part,
        real_part * sine_part + imag_part * cosine_part,
    )


def filter_window():
    sample_index = jnp.arange(TAPS * NCHAN, dtype=jnp.float32)
    centred = (sample_index - TAPS * NCHAN / 2 + 0.5) / NCHAN
    taper_curve = 0.5 - 0.5 * jnp.cos(full_turn * (sample_index + 0.5) / (TAPS * NCHAN))
    shaped_window = (jnp.sinc(centred) * taper_curve).reshape(TAPS, NCHAN)
    energy = jnp.mean(jnp.sum(shaped_window * shaped_window, axis=0))
    return shaped_window / jnp.sqrt(energy)


def channelize(framed, window, first_table, second_table, gains):
    frames = framed.shape[2] - TAPS + 1
    filtered = window[0] * framed[:, :, 0:frames]
    for tap_index in range(1, TAPS):
        filtered = filtered + window[tap_index] * framed[:, :, tap_index : tap_index + frames]
    filtered = filtered.astype(jnp.bfloat16)
    section_one = jnp.einsum(
        "rpfab,paqc->rfqcb", filtered, first_table, preferred_element_type=jnp.float32
    )
    first_index = jnp.arange(CHA, dtype=jnp.int32)
    second_index = jnp.arange(CHB, dtype=jnp.int32)
    angles = -(full_turn / NCHAN) * (first_index[:, None] * second_index[None, :] % NCHAN).astype(
        jnp.float32
    )
    real_part, imag_part = rotate(section_one[:, :, 0], section_one[:, :, 1], angles)
    turned = jnp.stack([real_part, imag_part], axis=2).astype(jnp.bfloat16)
    spectrum = jnp.einsum(
        "rfqcb,qbse->rfsec", turned, second_table, preferred_element_type=jnp.float32
    )
    spectrum_real = spectrum[:, :, 0]
    spectrum_imag = spectrum[:, :, 1]
    gain_real = gains[:, 0][:, None]
    gain_imag = gains[:, 1][:, None]
    out_real = spectrum_real * gain_real - spectrum_imag * gain_imag
    out_imag = spectrum_real * gain_imag + spectrum_imag * gain_real
    return jnp.stack([out_real, out_imag], axis=2).astype(jnp.bfloat16)


def beam_kernel(scale, x_ref, table_ref, twist_ref, power_ref):
    groups, _, _, _, rows, width = x_ref.shape
    positions = twist_ref.shape[2]
    parts = []
    for d in range(N_DISH):
        sums = None
        for p in range(2):
            feeds = x_ref[:, d, 0, p]
            if rows % 16:
                feeds = feeds.astype(jnp.float32).reshape(groups * rows, width).astype(jnp.bfloat16)
            else:
                feeds = feeds.reshape(groups * rows, width)
            term = lax.dot_general(
                feeds,
                table_ref[d, p],
                (((0,), (0,)), ((), ())),
                preferred_element_type=jnp.float32,
            )
            sums = term if sums is None else sums + term
        real, imag = sums[:, :positions], sums[:, positions:]
        cosine, sine = twist_ref[d, 0:1], twist_ref[d, 1:2]
        parts.append(
            (
                (real * cosine - imag * sine).astype(jnp.bfloat16).astype(jnp.float32),
                (real * sine + imag * cosine).astype(jnp.bfloat16).astype(jnp.float32),
            )
        )
    (r0, i0), (r1, i1), (r2, i2), (r3, i3) = parts
    ar, ai, br, bi = r0 + r2, i0 + i2, r1 + r3, i1 + i3
    cr, ci, dr, di = r0 - r2, i0 - i2, r1 - r3, i1 - i3
    beams = (
        (ar + br, ai + bi),
        (ar - br, ai - bi),
        (cr + di, ci - dr),
        (cr - di, ci + dr),
    )

    @pl.when(pl.program_id(0) == 0)
    def _():
        power_ref[...] = jnp.zeros_like(power_ref)

    for s, (real, imag) in enumerate(beams):
        power_ref[s] += (real * real + imag * imag) * scale


def beam_power(gathered, tables, twist):
    groups, dishes, frames, _, rows, width = gathered.shape
    positions = twist.shape[2]
    return pl.pallas_call(
        lambda *refs: beam_kernel(1.0 / (N_DISH * FRAMES), *refs),
        grid=(frames,),
        in_specs=[
            pl.BlockSpec((groups, dishes, 1, 2, rows, width), lambda f: (0, 0, f, 0, 0, 0)),
            pl.BlockSpec(tables.shape, lambda f: (0, 0, 0, 0)),
            pl.BlockSpec(twist.shape, lambda f: (0, 0, 0)),
        ],
        out_specs=pl.BlockSpec((N_DISH, width, positions), lambda f: (0, 0, 0)),
        out_shape=jax.ShapeDtypeStruct((N_DISH, width, positions), jnp.float32),
        compiler_params=pltpu.CompilerParams(vmem_limit_bytes=40 * 2**20),
        cost_estimate=pl.CostEstimate(
            flops=frames * dishes * groups * rows * 2 * width * positions * 4,
            bytes_accessed=gathered.size * 2 + tables.size * 2,
            transcendentals=0,
        ),
    )(gathered, tables, twist)


def body(voltages, feed_gains, block_assign, grid_rows):
    dish_rows = voltages.shape[0]
    block_count = lax.axis_size("freq")
    dish_count = lax.axis_size("dish")
    devices = block_count * dish_count
    block_width = NCHAN // block_count
    width = block_width // dish_count
    grid_len = grid_rows.shape[1]
    total_dishes = grid_len * dish_count

    window = filter_window().reshape(TAPS, CHA, CHB)
    first_index = jnp.arange(CHA, dtype=jnp.int32)
    second_index = jnp.arange(CHB, dtype=jnp.int32)
    first_table = fourier_table(first_index, first_index, CHA, 1.0 / math.sqrt(CHA))
    per_block = CHB // block_count
    ordered = (
        block_assign[:, None] * per_block + jnp.arange(per_block, dtype=jnp.int32)[None]
    ).reshape(CHB)
    second_table = fourier_table(second_index, ordered, CHB, 1.0 / math.sqrt(CHB))
    chosen = (jnp.arange(block_count)[:, None] == block_assign[None, :]).astype(jnp.bfloat16)
    gains = jnp.einsum(
        "rpbw,bn->rpnw",
        feed_gains[:, 0].reshape(dish_rows, 2, block_count, block_width),
        chosen,
        preferred_element_type=jnp.float32,
    ).reshape(dish_rows, 2, CHB, CHA)

    positions = jnp.arange(grid_len, dtype=jnp.int32)
    tables = jax.vmap(
        lambda line: fourier_table(line, positions, grid_len, 1.0 / math.sqrt(grid_len))
    )(grid_rows).reshape(dish_count, 2, grid_len, 2 * grid_len)
    classes = jnp.arange(dish_count, dtype=jnp.int32)
    twist_angles = -(full_turn / total_dishes) * (
        classes[:, None] * positions[None, :] % total_dishes
    ).astype(jnp.float32)
    twist = jnp.stack([jnp.cos(twist_angles), jnp.sin(twist_angles)], axis=1)

    framed = voltages[:, 0].reshape(dish_rows, 2, FRAMES + TAPS - 1, CHA, CHB)
    step = FRAMES // CHUNKS
    total = None
    for chunk in range(CHUNKS):
        piece = framed[:, :, chunk * step : chunk * step + step + TAPS - 1]
        spectra = channelize(piece, window, first_table, second_table, gains)
        spectra = spectra.reshape(dish_rows, step, 2, devices, width)
        sent = jnp.transpose(spectra, (3, 1, 2, 0, 4))
        gathered = lax.all_to_all(sent, ("freq", "dish"), split_axis=0, concat_axis=0, tiled=True)
        gathered = gathered.reshape(block_count, dish_count, step, 2, dish_rows, width)
        power = beam_power(gathered, tables, twist)
        total = power if total is None else total + power
    out = lax.all_to_all(total, "dish", split_axis=0, concat_axis=0, tiled=True)
    return out.reshape(block_width, grid_len)


def solution(mesh):
    placed = (P("freq", "dish", None, None), P("freq", "dish", None, None), P(), P())
    return jax.shard_map(
        body, mesh=mesh, in_specs=placed, out_specs=P("freq", "dish"), check_vma=False
    )
```

```python
import math

import jax
import jax.numpy as jnp
from jax import lax
from jax.experimental import pallas as pl
from jax.experimental.pallas import tpu as pltpu
from jax.sharding import PartitionSpec as P

NCHAN = 8192
CHA = 64
CHB = 128
TAPS = 4
FRAMES = 16
N_DISH = 4
CHUNKS = 4


full_turn = 2.0 * math.pi


def fourier_table(row_index, col_index, modulus, scaling):
    phases = row_index[:, None] * col_index[None, :] % modulus
    angles = full_turn / modulus * phases.astype(jnp.float32)
    cosine_table = (jnp.cos(angles) * scaling).astype(jnp.bfloat16)
    sine_table = (jnp.sin(angles) * scaling).astype(jnp.bfloat16)
    upper_rows = jnp.stack([cosine_table, -sine_table], axis=1)
    lower_rows = jnp.stack([sine_table, cosine_table], axis=1)
    return jnp.stack([upper_rows, lower_rows], axis=0)


def filter_window():
    sample_index = jnp.arange(TAPS * NCHAN, dtype=jnp.float32)
    centred = (sample_index - TAPS * NCHAN / 2 + 0.5) / NCHAN
    taper_curve = 0.5 - 0.5 * jnp.cos(full_turn * (sample_index + 0.5) / (TAPS * NCHAN))
    shaped_window = (jnp.sinc(centred) * taper_curve).reshape(TAPS, NCHAN)
    energy = jnp.mean(jnp.sum(shaped_window * shaped_window, axis=0))
    return shaped_window / jnp.sqrt(energy)


def channel_kernel(start, frames, v_ref, window_ref, first_ref, turn_ref, second_ref, gain_ref, out_ref):
    rows = []
    for f in range(frames):
        filtered = window_ref[0] * v_ref[0, start + f].astype(jnp.float32)
        for t in range(1, TAPS):
            filtered = filtered + window_ref[t] * v_ref[0, start + f + t].astype(jnp.float32)
        section = jnp.dot(
            first_ref[...], filtered.astype(jnp.bfloat16), preferred_element_type=jnp.float32
        )
        real, imag = section[:CHA], section[CHA:]
        cosine, sine = turn_ref[0], turn_ref[1]
        turned = jnp.concatenate(
            [real * cosine - imag * sine, real * sine + imag * cosine], axis=1
        )
        rows.append(turned.astype(jnp.bfloat16))
    spectrum = lax.dot_general(
        second_ref[...],
        jnp.concatenate(rows, axis=0),
        (((1,), (1,)), ((), ())),
        preferred_element_type=jnp.float32,
    )
    real, imag = spectrum[:CHB], spectrum[CHB:]
    gain_real = gain_ref[0, 0].astype(jnp.float32)
    gain_imag = gain_ref[0, 1].astype(jnp.float32)
    out_ref[0, 0] = (real * gain_real - imag * gain_imag).astype(jnp.bfloat16)
    out_ref[0, 1] = (real * gain_imag + imag * gain_real).astype(jnp.bfloat16)


def channelize(start, frames, volts, window, first_table, turn, second_table, gains):
    feeds = volts.shape[0]
    width = frames * CHA

    def whole(array):
        return pl.BlockSpec(array.shape, lambda r: (0,) * array.ndim)

    def own(array):
        return pl.BlockSpec((1,) + array.shape[1:], lambda r: (r,) + (0,) * (array.ndim - 1))

    out = jax.ShapeDtypeStruct((feeds, 2, CHB, width), jnp.bfloat16)
    return pl.pallas_call(
        lambda *refs: channel_kernel(start, frames, *refs),
        grid=(feeds,),
        in_specs=[
            own(volts),
            whole(window),
            whole(first_table),
            whole(turn),
            whole(second_table),
            own(gains),
        ],
        out_specs=own(out),
        out_shape=out,
        compiler_params=pltpu.CompilerParams(vmem_limit_bytes=32 * 2**20),
        cost_estimate=pl.CostEstimate(
            flops=feeds * frames * (2 * 128**3 + 2 * 64 * 256 * 256),
            bytes_accessed=volts.size * 2 + gains.size * 2 + feeds * 512 * width,
            transcendentals=0,
        ),
    )(volts, window, first_table, turn, second_table, gains)


def beam_kernel(scale, x_ref, table_ref, twist_ref, power_ref):
    groups, _, _, _, rows, width = x_ref.shape
    frames = width // CHA
    positions = twist_ref.shape[2]
    parts = []
    for d in range(N_DISH):
        sums = None
        for p in range(2):
            feeds = x_ref[:, d, p, 0]
            if rows % 16:
                feeds = feeds.astype(jnp.float32).reshape(groups * rows, width).astype(jnp.bfloat16)
            else:
                feeds = feeds.reshape(groups * rows, width)
            term = lax.dot_general(
                feeds,
                table_ref[d, p],
                (((0,), (0,)), ((), ())),
                preferred_element_type=jnp.float32,
            )
            sums = term if sums is None else sums + term
        real, imag = sums[:, :positions], sums[:, positions:]
        cosine, sine = twist_ref[d, 0:1], twist_ref[d, 1:2]
        parts.append(
            (
                (real * cosine - imag * sine).astype(jnp.bfloat16).astype(jnp.float32),
                (real * sine + imag * cosine).astype(jnp.bfloat16).astype(jnp.float32),
            )
        )
    (r0, i0), (r1, i1), (r2, i2), (r3, i3) = parts
    ar, ai, br, bi = r0 + r2, i0 + i2, r1 + r3, i1 + i3
    cr, ci, dr, di = r0 - r2, i0 - i2, r1 - r3, i1 - i3
    beams = (
        (ar + br, ai + bi),
        (ar - br, ai - bi),
        (cr + di, ci - dr),
        (cr - di, ci + dr),
    )

    for s, (real, imag) in enumerate(beams):
        power = (real * real + imag * imag) * scale
        power_ref[s] = sum(power[f * CHA : (f + 1) * CHA] for f in range(frames))


def beam_power(gathered, tables, twist):
    groups, dishes, _, parts, rows, width = gathered.shape
    positions = twist.shape[2]
    return pl.pallas_call(
        lambda *refs: beam_kernel(1.0 / (N_DISH * FRAMES), *refs),
        grid=(parts,),
        in_specs=[
            pl.BlockSpec((groups, dishes, 2, 1, rows, width), lambda e: (0, 0, 0, e, 0, 0)),
            pl.BlockSpec(tables.shape, lambda e: (0, 0, 0, 0)),
            pl.BlockSpec(twist.shape, lambda e: (0, 0, 0)),
        ],
        out_specs=pl.BlockSpec((N_DISH, CHA, positions), lambda e: (0, e, 0)),
        out_shape=jax.ShapeDtypeStruct((N_DISH, parts * CHA, positions), jnp.float32),
        compiler_params=pltpu.CompilerParams(vmem_limit_bytes=40 * 2**20),
        cost_estimate=pl.CostEstimate(
            flops=parts * dishes * groups * rows * 2 * width * positions * 4,
            bytes_accessed=gathered.size * 2 + tables.size * 2,
            transcendentals=0,
        ),
    )(gathered, tables, twist)


def body(voltages, feed_gains, block_assign, grid_rows):
    dish_rows = voltages.shape[0]
    block_count = lax.axis_size("freq")
    dish_count = lax.axis_size("dish")
    devices = block_count * dish_count
    block_width = NCHAN // block_count
    parts = CHB // devices
    grid_len = grid_rows.shape[1]
    total_dishes = grid_len * dish_count

    step = FRAMES // CHUNKS
    window = jnp.repeat(filter_window().reshape(TAPS, CHA, CHB), 2, axis=1)
    first_index = jnp.arange(CHA, dtype=jnp.int32)
    second_index = jnp.arange(CHB, dtype=jnp.int32)
    first_table = fourier_table(first_index, first_index, CHA, 1.0 / math.sqrt(CHA))
    first_table = jnp.transpose(first_table, (2, 3, 1, 0)).reshape(2 * CHA, 2 * CHA)
    turn_angles = -(full_turn / NCHAN) * (
        first_index[:, None] * second_index[None, :] % NCHAN
    ).astype(jnp.float32)
    turn = jnp.stack([jnp.cos(turn_angles), jnp.sin(turn_angles)])
    per_block = CHB // block_count
    ordered = (
        block_assign[:, None] * per_block + jnp.arange(per_block, dtype=jnp.int32)[None]
    ).reshape(CHB)
    second_table = fourier_table(second_index, ordered, CHB, 1.0 / math.sqrt(CHB))
    second_table = jnp.transpose(second_table, (2, 3, 0, 1)).reshape(2 * CHB, 2 * CHB)
    chosen = (jnp.arange(block_count)[:, None] == block_assign[None, :]).astype(jnp.bfloat16)
    gains = jnp.einsum(
        "rpbw,bn->rpnw",
        feed_gains[:, 0].reshape(dish_rows, 2, block_count, block_width),
        chosen,
        preferred_element_type=jnp.float32,
    ).reshape(dish_rows, 2, CHB, CHA)
    gains = jnp.tile(gains.astype(jnp.bfloat16), (1, 1, 1, step))

    positions = jnp.arange(grid_len, dtype=jnp.int32)
    tables = jax.vmap(
        lambda line: fourier_table(line, positions, grid_len, 1.0 / math.sqrt(grid_len))
    )(grid_rows).reshape(dish_count, 2, grid_len, 2 * grid_len)
    classes = jnp.arange(dish_count, dtype=jnp.int32)
    twist_angles = -(full_turn / total_dishes) * (
        classes[:, None] * positions[None, :] % total_dishes
    ).astype(jnp.float32)
    twist = jnp.stack([jnp.cos(twist_angles), jnp.sin(twist_angles)], axis=1)

    spans = FRAMES + TAPS - 1
    volts = voltages[:, 0].reshape(dish_rows, 2, spans * CHA, CHB)
    volts = jnp.transpose(volts, (0, 2, 1, 3)).reshape(dish_rows, spans, 2 * CHA, CHB)
    total = None
    for chunk in range(CHUNKS):
        spectra = channelize(
            chunk * step, step, volts, window, first_table, turn, second_table, gains
        )
        spectra = spectra.reshape(dish_rows, 2, devices, parts, step * CHA)
        sent = jnp.transpose(spectra, (2, 1, 3, 0, 4))
        sent, first_table = lax.optimization_barrier((sent, first_table))
        gathered = lax.all_to_all(sent, ("freq", "dish"), split_axis=0, concat_axis=0, tiled=True)
        gathered = gathered.reshape(block_count, dish_count, 2, parts, dish_rows, step * CHA)
        power = beam_power(gathered, tables, twist)
        total = power if total is None else total + power
    out = lax.all_to_all(total, "dish", split_axis=0, concat_axis=0, tiled=True)
    return out.reshape(block_width, grid_len)


def solution(mesh):
    placed = (P("freq", "dish", None, None), P("freq", "dish", None, None), P(), P())
    return jax.shard_map(
        body, mesh=mesh, in_specs=placed, out_specs=P("freq", "dish"), check_vma=False
    )
```

```python
import math

import jax
import jax.numpy as jnp
from jax import lax
from jax.experimental import pallas as pl
from jax.experimental.pallas import tpu as pltpu
from jax.sharding import PartitionSpec as P

NCHAN = 8192
CHA = 64
CHB = 128
TAPS = 4
FRAMES = 16
N_DISH = 4
CHUNKS = (2, 4, 8, 2)


full_turn = 2.0 * math.pi


def fourier_table(row_index, col_index, modulus, scaling):
    phases = row_index[:, None] * col_index[None, :] % modulus
    angles = full_turn / modulus * phases.astype(jnp.float32)
    cosine_table = (jnp.cos(angles) * scaling).astype(jnp.bfloat16)
    sine_table = (jnp.sin(angles) * scaling).astype(jnp.bfloat16)
    upper_rows = jnp.stack([cosine_table, -sine_table], axis=1)
    lower_rows = jnp.stack([sine_table, cosine_table], axis=1)
    return jnp.stack([upper_rows, lower_rows], axis=0)


def filter_window():
    sample_index = jnp.arange(TAPS * NCHAN, dtype=jnp.float32)
    centred = (sample_index - TAPS * NCHAN / 2 + 0.5) / NCHAN
    taper_curve = 0.5 - 0.5 * jnp.cos(full_turn * (sample_index + 0.5) / (TAPS * NCHAN))
    shaped_window = (jnp.sinc(centred) * taper_curve).reshape(TAPS, NCHAN)
    energy = jnp.mean(jnp.sum(shaped_window * shaped_window, axis=0))
    return shaped_window / jnp.sqrt(energy)


def channel_kernel(start, frames, v_ref, window_ref, first_ref, turn_ref, second_ref, gain_ref, out_ref):
    rows = []
    for f in range(frames):
        filtered = window_ref[0] * v_ref[0, start + f].astype(jnp.float32)
        for t in range(1, TAPS):
            filtered = filtered + window_ref[t] * v_ref[0, start + f + t].astype(jnp.float32)
        section = jnp.dot(
            first_ref[...], filtered.astype(jnp.bfloat16), preferred_element_type=jnp.float32
        )
        real, imag = section[:CHA], section[CHA:]
        cosine, sine = turn_ref[0], turn_ref[1]
        turned = jnp.concatenate(
            [real * cosine - imag * sine, real * sine + imag * cosine], axis=1
        )
        rows.append(turned.astype(jnp.bfloat16))
    spectrum = lax.dot_general(
        second_ref[...],
        jnp.concatenate(rows, axis=0),
        (((1,), (1,)), ((), ())),
        preferred_element_type=jnp.float32,
    )
    real, imag = spectrum[:CHB], spectrum[CHB:]
    gain_real = jnp.concatenate([gain_ref[0, 0].astype(jnp.float32)] * frames, axis=1)
    gain_imag = jnp.concatenate([gain_ref[0, 1].astype(jnp.float32)] * frames, axis=1)
    out_ref[0, 0] = (real * gain_real - imag * gain_imag).astype(jnp.bfloat16)
    out_ref[0, 1] = (real * gain_imag + imag * gain_real).astype(jnp.bfloat16)


def channelize(start, frames, volts, window, first_table, turn, second_table, gains):
    feeds = volts.shape[0]
    width = frames * CHA

    def whole(array):
        return pl.BlockSpec(array.shape, lambda r: (0,) * array.ndim)

    def own(array):
        return pl.BlockSpec((1,) + array.shape[1:], lambda r: (r,) + (0,) * (array.ndim - 1))

    out = jax.ShapeDtypeStruct((feeds, 2, CHB, width), jnp.bfloat16)
    return pl.pallas_call(
        lambda *refs: channel_kernel(start, frames, *refs),
        grid=(feeds,),
        in_specs=[
            own(volts),
            whole(window),
            whole(first_table),
            whole(turn),
            whole(second_table),
            own(gains),
        ],
        out_specs=own(out),
        out_shape=out,
        compiler_params=pltpu.CompilerParams(vmem_limit_bytes=32 * 2**20),
        cost_estimate=pl.CostEstimate(
            flops=feeds * frames * (2 * 128**3 + 2 * 64 * 256 * 256),
            bytes_accessed=volts.size * 2 + gains.size * 2 + feeds * 512 * width,
            transcendentals=0,
        ),
    )(volts, window, first_table, turn, second_table, gains)


def beam_kernel(scale, x_ref, table_ref, twist_ref, power_ref):
    groups, _, _, _, rows, width = x_ref.shape
    frames = width // CHA
    positions = twist_ref.shape[2]
    parts = []
    for d in range(N_DISH):
        sums = None
        for p in range(2):
            feeds = x_ref[:, d, p, 0]
            if rows % 16:
                feeds = feeds.astype(jnp.float32).reshape(groups * rows, width).astype(jnp.bfloat16)
            else:
                feeds = feeds.reshape(groups * rows, width)
            term = lax.dot_general(
                feeds,
                table_ref[d, p],
                (((0,), (0,)), ((), ())),
                preferred_element_type=jnp.float32,
            )
            sums = term if sums is None else sums + term
        real, imag = sums[:, :positions], sums[:, positions:]
        cosine, sine = twist_ref[d, 0:1], twist_ref[d, 1:2]
        parts.append(
            (
                (real * cosine - imag * sine).astype(jnp.bfloat16).astype(jnp.float32),
                (real * sine + imag * cosine).astype(jnp.bfloat16).astype(jnp.float32),
            )
        )
    (r0, i0), (r1, i1), (r2, i2), (r3, i3) = parts
    ar, ai, br, bi = r0 + r2, i0 + i2, r1 + r3, i1 + i3
    cr, ci, dr, di = r0 - r2, i0 - i2, r1 - r3, i1 - i3
    beams = (
        (ar + br, ai + bi),
        (ar - br, ai - bi),
        (cr + di, ci - dr),
        (cr - di, ci + dr),
    )

    for s, (real, imag) in enumerate(beams):
        power = (real * real + imag * imag) * scale
        power_ref[s] = sum(power[f * CHA : (f + 1) * CHA] for f in range(frames))


def beam_power(gathered, tables, twist):
    groups, dishes, _, parts, rows, width = gathered.shape
    positions = twist.shape[2]
    return pl.pallas_call(
        lambda *refs: beam_kernel(1.0 / (N_DISH * FRAMES), *refs),
        grid=(parts,),
        in_specs=[
            pl.BlockSpec((groups, dishes, 2, 1, rows, width), lambda e: (0, 0, 0, e, 0, 0)),
            pl.BlockSpec(tables.shape, lambda e: (0, 0, 0, 0)),
            pl.BlockSpec(twist.shape, lambda e: (0, 0, 0)),
        ],
        out_specs=pl.BlockSpec((N_DISH, CHA, positions), lambda e: (0, e, 0)),
        out_shape=jax.ShapeDtypeStruct((N_DISH, parts * CHA, positions), jnp.float32),
        compiler_params=pltpu.CompilerParams(vmem_limit_bytes=40 * 2**20),
        cost_estimate=pl.CostEstimate(
            flops=parts * dishes * groups * rows * 2 * width * positions * 4,
            bytes_accessed=gathered.size * 2 + tables.size * 2,
            transcendentals=0,
        ),
    )(gathered, tables, twist)


def body(voltages, feed_gains, block_assign, grid_rows):
    dish_rows = voltages.shape[0]
    block_count = lax.axis_size("freq")
    dish_count = lax.axis_size("dish")
    devices = block_count * dish_count
    block_width = NCHAN // block_count
    parts = CHB // devices
    grid_len = grid_rows.shape[1]
    total_dishes = grid_len * dish_count

    window = jnp.repeat(filter_window().reshape(TAPS, CHA, CHB), 2, axis=1)
    first_index = jnp.arange(CHA, dtype=jnp.int32)
    second_index = jnp.arange(CHB, dtype=jnp.int32)
    first_table = fourier_table(first_index, first_index, CHA, 1.0 / math.sqrt(CHA))
    first_table = jnp.transpose(first_table, (2, 3, 1, 0)).reshape(2 * CHA, 2 * CHA)
    turn_angles = -(full_turn / NCHAN) * (
        first_index[:, None] * second_index[None, :] % NCHAN
    ).astype(jnp.float32)
    turn = jnp.stack([jnp.cos(turn_angles), jnp.sin(turn_angles)])
    per_block = CHB // block_count
    ordered = (
        block_assign[:, None] * per_block + jnp.arange(per_block, dtype=jnp.int32)[None]
    ).reshape(CHB)
    second_table = fourier_table(second_index, ordered, CHB, 1.0 / math.sqrt(CHB))
    second_table = jnp.transpose(second_table, (2, 3, 0, 1)).reshape(2 * CHB, 2 * CHB)
    chosen = (jnp.arange(block_count)[:, None] == block_assign[None, :]).astype(jnp.bfloat16)
    gains = jnp.einsum(
        "rpbw,bn->rpnw",
        feed_gains[:, 0].reshape(dish_rows, 2, block_count, block_width),
        chosen,
        preferred_element_type=jnp.float32,
    ).reshape(dish_rows, 2, CHB, CHA)
    gains = gains.astype(jnp.bfloat16)

    positions = jnp.arange(grid_len, dtype=jnp.int32)
    tables = jax.vmap(
        lambda line: fourier_table(line, positions, grid_len, 1.0 / math.sqrt(grid_len))
    )(grid_rows).reshape(dish_count, 2, grid_len, 2 * grid_len)
    classes = jnp.arange(dish_count, dtype=jnp.int32)
    twist_angles = -(full_turn / total_dishes) * (
        classes[:, None] * positions[None, :] % total_dishes
    ).astype(jnp.float32)
    twist = jnp.stack([jnp.cos(twist_angles), jnp.sin(twist_angles)], axis=1)

    spans = FRAMES + TAPS - 1
    volts = voltages[:, 0].reshape(dish_rows, 2, spans * CHA, CHB)
    volts = jnp.transpose(volts, (0, 2, 1, 3)).reshape(dish_rows, spans, 2 * CHA, CHB)
    total = None
    arrived = None
    start = 0
    for step in CHUNKS:
        spectra = channelize(
            start, step, volts, window, first_table, turn, second_table, gains
        )
        start += step
        spectra = spectra.reshape(dish_rows, 2, devices, parts, step * CHA)
        sent = jnp.transpose(spectra, (2, 1, 3, 0, 4))
        if arrived is None:
            sent, first_table = lax.optimization_barrier((sent, first_table))
        else:
            sent, first_table, arrived = lax.optimization_barrier((sent, first_table, arrived))
            power = beam_power(arrived, tables, twist)
            total = power if total is None else total + power
        gathered = lax.all_to_all(sent, ("freq", "dish"), split_axis=0, concat_axis=0, tiled=True)
        arrived = gathered.reshape(block_count, dish_count, 2, parts, dish_rows, step * CHA)
    total = total + beam_power(arrived, tables, twist)
    total = total.astype(jnp.bfloat16)
    out = lax.all_to_all(total, "dish", split_axis=0, concat_axis=0, tiled=True)
    return out.reshape(block_width, grid_len).astype(jnp.float32)


def solution(mesh):
    placed = (P("freq", "dish", None, None), P("freq", "dish", None, None), P(), P())
    return jax.shard_map(
        body, mesh=mesh, in_specs=placed, out_specs=P("freq", "dish"), check_vma=False
    )
```

```python
import math

import jax
import jax.numpy as jnp
from jax import lax
from jax.experimental import pallas as pl
from jax.experimental.pallas import tpu as pltpu
from jax.sharding import PartitionSpec as P

NCHAN = 8192
CHA = 64
CHB = 128
TAPS = 4
FRAMES = 16
N_DISH = 4
CHUNKS = (2, 4, 8, 2)


full_turn = 2.0 * math.pi


def fourier_table(row_index, col_index, modulus, scaling):
    phases = row_index[:, None] * col_index[None, :] % modulus
    angles = full_turn / modulus * phases.astype(jnp.float32)
    cosine_table = (jnp.cos(angles) * scaling).astype(jnp.bfloat16)
    sine_table = (jnp.sin(angles) * scaling).astype(jnp.bfloat16)
    upper_rows = jnp.stack([cosine_table, -sine_table], axis=1)
    lower_rows = jnp.stack([sine_table, cosine_table], axis=1)
    return jnp.stack([upper_rows, lower_rows], axis=0)


def filter_window():
    sample_index = jnp.arange(TAPS * NCHAN, dtype=jnp.float32)
    centred = (sample_index - TAPS * NCHAN / 2 + 0.5) / NCHAN
    taper_curve = 0.5 - 0.5 * jnp.cos(full_turn * (sample_index + 0.5) / (TAPS * NCHAN))
    shaped_window = (jnp.sinc(centred) * taper_curve).reshape(TAPS, NCHAN)
    energy = jnp.mean(jnp.sum(shaped_window * shaped_window, axis=0))
    return shaped_window / jnp.sqrt(energy)


def channel_kernel(start, frames, v_ref, window_ref, first_ref, turn_ref, second_ref, gain_ref, out_ref):
    rows = []
    for f in range(frames):
        filtered = window_ref[0] * v_ref[0, start + f].astype(jnp.float32)
        for t in range(1, TAPS):
            filtered = filtered + window_ref[t] * v_ref[0, start + f + t].astype(jnp.float32)
        section = jnp.dot(
            first_ref[...], filtered.astype(jnp.bfloat16), preferred_element_type=jnp.float32
        )
        real, imag = section[:CHA], section[CHA:]
        cosine, sine = turn_ref[0], turn_ref[1]
        turned = jnp.concatenate(
            [real * cosine - imag * sine, real * sine + imag * cosine], axis=1
        )
        rows.append(turned.astype(jnp.bfloat16))
    spectrum = lax.dot_general(
        second_ref[...],
        jnp.concatenate(rows, axis=0),
        (((1,), (1,)), ((), ())),
        preferred_element_type=jnp.float32,
    )
    real, imag = spectrum[:CHB], spectrum[CHB:]
    gain_real = jnp.concatenate([gain_ref[0, 0].astype(jnp.float32)] * frames, axis=1)
    gain_imag = jnp.concatenate([gain_ref[0, 1].astype(jnp.float32)] * frames, axis=1)
    out_ref[0, 0] = (real * gain_real - imag * gain_imag).astype(jnp.bfloat16)
    out_ref[0, 1] = (real * gain_imag + imag * gain_real).astype(jnp.bfloat16)


def channelize(start, frames, volts, window, first_table, turn, second_table, gains):
    feeds = volts.shape[0]
    width = frames * CHA

    def whole(array):
        return pl.BlockSpec(array.shape, lambda r: (0,) * array.ndim)

    def own(array):
        return pl.BlockSpec((1,) + array.shape[1:], lambda r: (r,) + (0,) * (array.ndim - 1))

    out = jax.ShapeDtypeStruct((feeds, 2, CHB, width), jnp.bfloat16)
    return pl.pallas_call(
        lambda *refs: channel_kernel(start, frames, *refs),
        grid=(feeds,),
        in_specs=[
            pl.BlockSpec(
                (1, start + frames + TAPS - 1) + volts.shape[2:], lambda r: (r, 0, 0, 0)
            ),
            whole(window),
            whole(first_table),
            whole(turn),
            whole(second_table),
            own(gains),
        ],
        out_specs=own(out),
        out_shape=out,
        compiler_params=pltpu.CompilerParams(vmem_limit_bytes=32 * 2**20),
        cost_estimate=pl.CostEstimate(
            flops=feeds * frames * (2 * 128**3 + 2 * 64 * 256 * 256),
            bytes_accessed=feeds * (start + frames + 3) * 2**15 + gains.size * 2 + feeds * 512 * width,
            transcendentals=0,
        ),
    )(volts, window, first_table, turn, second_table, gains)


def beam_kernel(scale, x_ref, table_ref, twist_ref, power_ref):
    groups, _, _, _, rows, width = x_ref.shape
    frames = width // CHA
    positions = twist_ref.shape[2]
    parts = []
    for d in range(N_DISH):
        sums = None
        for p in range(2):
            feeds = x_ref[:, d, p, 0]
            if rows % 16:
                feeds = feeds.astype(jnp.float32).reshape(groups * rows, width).astype(jnp.bfloat16)
            else:
                feeds = feeds.reshape(groups * rows, width)
            term = lax.dot_general(
                feeds,
                table_ref[d, p],
                (((0,), (0,)), ((), ())),
                preferred_element_type=jnp.float32,
            )
            sums = term if sums is None else sums + term
        real, imag = sums[:, :positions], sums[:, positions:]
        cosine, sine = twist_ref[d, 0:1], twist_ref[d, 1:2]
        parts.append(
            (
                (real * cosine - imag * sine).astype(jnp.bfloat16).astype(jnp.float32),
                (real * sine + imag * cosine).astype(jnp.bfloat16).astype(jnp.float32),
            )
        )
    (r0, i0), (r1, i1), (r2, i2), (r3, i3) = parts
    ar, ai, br, bi = r0 + r2, i0 + i2, r1 + r3, i1 + i3
    cr, ci, dr, di = r0 - r2, i0 - i2, r1 - r3, i1 - i3
    beams = (
        (ar + br, ai + bi),
        (ar - br, ai - bi),
        (cr + di, ci - dr),
        (cr - di, ci + dr),
    )

    for s, (real, imag) in enumerate(beams):
        power = (real * real + imag * imag) * scale
        power_ref[s] = sum(power[f * CHA : (f + 1) * CHA] for f in range(frames))


def beam_power(gathered, tables, twist):
    groups, dishes, _, parts, rows, width = gathered.shape
    positions = twist.shape[2]
    return pl.pallas_call(
        lambda *refs: beam_kernel(1.0 / (N_DISH * FRAMES), *refs),
        grid=(parts,),
        in_specs=[
            pl.BlockSpec((groups, dishes, 2, 1, rows, width), lambda e: (0, 0, 0, e, 0, 0)),
            pl.BlockSpec(tables.shape, lambda e: (0, 0, 0, 0)),
            pl.BlockSpec(twist.shape, lambda e: (0, 0, 0)),
        ],
        out_specs=pl.BlockSpec((N_DISH, CHA, positions), lambda e: (0, e, 0)),
        out_shape=jax.ShapeDtypeStruct((N_DISH, parts * CHA, positions), jnp.float32),
        compiler_params=pltpu.CompilerParams(vmem_limit_bytes=40 * 2**20),
        cost_estimate=pl.CostEstimate(
            flops=parts * dishes * groups * rows * 2 * width * positions * 4,
            bytes_accessed=gathered.size * 2 + tables.size * 2,
            transcendentals=0,
        ),
    )(gathered, tables, twist)


def body(voltages, feed_gains, block_assign, grid_rows):
    dish_rows = voltages.shape[0]
    block_count = lax.axis_size("freq")
    dish_count = lax.axis_size("dish")
    devices = block_count * dish_count
    block_width = NCHAN // block_count
    parts = CHB // devices
    grid_len = grid_rows.shape[1]
    total_dishes = grid_len * dish_count

    window = jnp.repeat(filter_window().reshape(TAPS, CHA, CHB), 2, axis=1)
    first_index = jnp.arange(CHA, dtype=jnp.int32)
    second_index = jnp.arange(CHB, dtype=jnp.int32)
    first_table = fourier_table(first_index, first_index, CHA, 1.0 / math.sqrt(CHA))
    first_table = jnp.transpose(first_table, (2, 3, 1, 0)).reshape(2 * CHA, 2 * CHA)
    turn_angles = -(full_turn / NCHAN) * (
        first_index[:, None] * second_index[None, :] % NCHAN
    ).astype(jnp.float32)
    turn = jnp.stack([jnp.cos(turn_angles), jnp.sin(turn_angles)])
    per_block = CHB // block_count
    ordered = (
        block_assign[:, None] * per_block + jnp.arange(per_block, dtype=jnp.int32)[None]
    ).reshape(CHB)
    second_table = fourier_table(second_index, ordered, CHB, 1.0 / math.sqrt(CHB))
    second_table = jnp.transpose(second_table, (2, 3, 0, 1)).reshape(2 * CHB, 2 * CHB)
    chosen = (jnp.arange(block_count)[:, None] == block_assign[None, :]).astype(jnp.bfloat16)
    gains = jnp.einsum(
        "rpbw,bn->rpnw",
        feed_gains[:, 0].reshape(dish_rows, 2, block_count, block_width),
        chosen,
        preferred_element_type=jnp.float32,
    ).reshape(dish_rows, 2, CHB, CHA)
    gains = gains.astype(jnp.bfloat16)

    positions = jnp.arange(grid_len, dtype=jnp.int32)
    tables = jax.vmap(
        lambda line: fourier_table(line, positions, grid_len, 1.0 / math.sqrt(grid_len))
    )(grid_rows).reshape(dish_count, 2, grid_len, 2 * grid_len)
    classes = jnp.arange(dish_count, dtype=jnp.int32)
    twist_angles = -(full_turn / total_dishes) * (
        classes[:, None] * positions[None, :] % total_dishes
    ).astype(jnp.float32)
    twist = jnp.stack([jnp.cos(twist_angles), jnp.sin(twist_angles)], axis=1)

    spans = FRAMES + TAPS - 1
    volts = voltages[:, 0].reshape(dish_rows, 2, spans * CHA, CHB)
    volts = jnp.transpose(volts, (0, 2, 1, 3)).reshape(dish_rows, spans, 2 * CHA, CHB)
    total = None
    arrived = None
    start = 0
    for step in CHUNKS:
        spectra = channelize(
            start, step, volts, window, first_table, turn, second_table, gains
        )
        start += step
        spectra = spectra.reshape(dish_rows, 2, devices, parts, step * CHA)
        sent = jnp.transpose(spectra, (2, 1, 3, 0, 4))
        if arrived is None:
            sent, first_table = lax.optimization_barrier((sent, first_table))
        else:
            sent, first_table, arrived = lax.optimization_barrier((sent, first_table, arrived))
            power = beam_power(arrived, tables, twist)
            total = power if total is None else total + power
        gathered = lax.all_to_all(sent, ("freq", "dish"), split_axis=0, concat_axis=0, tiled=True)
        arrived = gathered.reshape(block_count, dish_count, 2, parts, dish_rows, step * CHA)
    total = total + beam_power(arrived, tables, twist)
    total = total.astype(jnp.bfloat16)
    out = lax.all_to_all(total, "dish", split_axis=0, concat_axis=0, tiled=True)
    return out.reshape(block_width, grid_len).astype(jnp.float32)


def solution(mesh):
    placed = (P("freq", "dish", None, None), P("freq", "dish", None, None), P(), P())
    return jax.shard_map(
        body, mesh=mesh, in_specs=placed, out_specs=P("freq", "dish"), check_vma=False
    )
```
